32 devices in a mesh: groups: 1, tensor: 32 (over z, y, x, core), dp: 1.
Axes of the slice: x: 2, y: 2, z: 4, core: 2. Of those that a mesh axis runs over, the one named last changes fastest.
Arguments:
- layer_input: bfloat16 [256, 8192], P(('groups', 'dp'), 'tensor'), may hold values from -180 to 180
- out_grad: bfloat16 [256, 8192], P(('groups', 'dp'), 'tensor'), may hold values from -6 to 6
- norm_gain: float32 [8192], replicated, may hold values from 0.25 to 1.75
- w_gate: bfloat16 [8192, 3584], P('dp', 'tensor'), may hold values from -0.0625 to 0.0625
- w_up: bfloat16 [8192, 3584], P('dp', 'tensor'), may hold values from -0.0625 to 0.0625
- w_down: bfloat16 [3584, 8192], P('tensor', 'dp'), may hold values from -0.09375 to 0.09375
- pin_gate: bfloat16 [8192, 64], P('tensor'), may hold values from -0.0625 to 0.0625
- pin_up: bfloat16 [8192, 64], P('tensor'), may hold values from -0.0625 to 0.0625
- pout_gate: bfloat16 [3584, 64], P('tensor'), may hold values from -0.09375 to 0.09375
- pout_up: bfloat16 [3584, 64], P('tensor'), may hold values from -0.09375 to 0.09375
- pin_down: bfloat16 [3584, 64], P('tensor'), may hold values from -0.09375 to 0.09375
- pout_down: bfloat16 [8192, 64], P('tensor'), may hold values from -0.0625 to 0.0625
- targets: float32 [1024, 12288], P('tensor'), may hold values from -0.0546875 to 0.0546875
Outputs:
- features: float32 [4, 12288], P(('groups', 'dp'))
- scores: float32 [4, 1024], P(('groups', 'dp'), 'tensor')
The draws below stay inside these ranges and needn't reach their ends.
All inputs are finite; a program needn't handle non-finite values.
Results may differ from the reference program's by a relative error of at most 0.0052.
Values may be sent and summed in bfloat16 or wider, within the bound.
A program may use at most 64 MiB of HBM per device.

```python
import math
import jax
import jax.numpy as jnp
from jax import lax

D = 8192
RANK = 64
SEQ = 64
FFN = 3584
TOKENS = 256
NTARGET = 1024
FEATS = 12288


def draw_layer_input(key, part):
    key_base = jax.random.fold_in(key, 11)
    key_rough = jax.random.fold_in(key, 12)
    key_rows = jax.random.fold_in(key, 13)
    column_pos = jnp.arange(D, dtype=jnp.float32) / D
    base = jax.random.truncated_normal(key_base, -4.0, 4.0, (TOKENS, D), jnp.float32)
    column_scale = jnp.exp(column_pos * 0.5 * math.log(3.0))
    rough = jax.random.uniform(key_rough, (1, D), jnp.float32, 0.5, 1.5)
    row_scale = jnp.exp(jax.random.uniform(key_rows, (TOKENS, 1), jnp.float32, 0.0, math.log(10.0)))
    return (base * column_scale * rough * row_scale).astype(jnp.bfloat16)


def block_scale(stream_key, dims, split, low, high):
    gain = 1.0
    for position, blocks in split:
        heights = jax.random.uniform(jax.random.fold_in(jax.random.fold_in(stream_key, 6), position), (blocks,), jnp.float32, low / len(split), high / len(split))
        gain = gain * jnp.repeat(jnp.exp(heights), dims[position] // blocks).reshape((-1,) + (1,) * (len(dims) - 1 - position))
    return gain


def centred(key, shape, spread, bound, split=(), kind=jnp.bfloat16):
    drawn = spread * jax.random.normal(key, shape, jnp.float32)
    if split:
        drawn = drawn * block_scale(key, shape, split, -0.22, 0.18)
    return jnp.clip(drawn, -bound, bound).astype(kind)


def setup_inputs(seed: int = 0, part: int = 0) -> dict:
    splits = jax.random.split(jax.random.key(seed), 14)
    part_keys = jax.random.split(jax.random.fold_in(splits[13], part), 14)
    return {
        "layer_input": draw_layer_input(jax.random.fold_in(jax.random.fold_in(splits[13], part), 71), part),
        "out_grad": centred(part_keys[1], (TOKENS, D), 1.0, 6.0, ((1, 32),)),
        "norm_gain": jnp.clip(1.0 + 0.15 * jax.random.normal(splits[2], (D,), jnp.float32), 0.25, 1.75),
        "w_gate": centred(splits[3], (D, FFN), D ** -0.5, 0.0625, ((1, 32),)),
        "w_up": centred(splits[4], (D, FFN), D ** -0.5, 0.0625, ((1, 32),)),
        "w_down": centred(splits[5], (FFN, D), FFN ** -0.5, 0.09375, ((0, 32),)),
        "pin_gate": centred(splits[6], (D, RANK), D ** -0.5, 0.0625, ((0, 32),)),
        "pin_up": centred(splits[7], (D, RANK), D ** -0.5, 0.0625, ((0, 32),)),
        "pout_gate": centred(splits[8], (FFN, RANK), FFN ** -0.5, 0.09375, ((0, 32),)),
        "pout_up": centred(splits[9], (FFN, RANK), FFN ** -0.5, 0.09375, ((0, 32),)),
        "pin_down": centred(splits[10], (FFN, RANK), FFN ** -0.5, 0.09375, ((0, 32),)),
        "pout_down": centred(splits[11], (D, RANK), D ** -0.5, 0.0625, ((0, 32),)),
        "targets": centred(splits[12], (NTARGET, FEATS), FEATS ** -0.5, 0.0546875, ((0, 32),), jnp.float32),
    }


EPSILON = 1e-05

def project_pair(out_side, in_side):
    out_rows = out_side.reshape(-1, SEQ, out_side.shape[-1])
    in_rows = in_side.reshape(-1, SEQ, in_side.shape[-1])
    product = jnp.einsum('esi,esj->eij', out_rows, in_rows, precision=lax.Precision.HIGHEST)
    return product.reshape(product.shape[0], -1)

def reference(layer_input, out_grad, norm_gain, w_gate, w_up, w_down, pin_gate, pin_up, pout_gate, pout_up, pin_down, pout_down, targets):
    wide_input = layer_input.astype(jnp.float32)
    mean_square = lax.optimization_barrier(jnp.mean(wide_input * wide_input, axis=-1, keepdims=True))
    normed = (wide_input * lax.rsqrt(mean_square + EPSILON) * norm_gain).astype(jnp.bfloat16)
    gate_pre = jnp.dot(normed, w_gate, preferred_element_type=jnp.float32)
    up_pre = jnp.dot(normed, w_up, preferred_element_type=jnp.float32)
    sigmoid_gate = jax.nn.sigmoid(gate_pre)
    activated = gate_pre * sigmoid_gate
    hidden_act = (activated * up_pre).astype(jnp.bfloat16)
    grad_hidden = jnp.dot(out_grad, w_down.T, preferred_element_type=jnp.float32)
    grad_gate = (grad_hidden * up_pre * sigmoid_gate * (1.0 + gate_pre * (1.0 - sigmoid_gate))).astype(jnp.bfloat16)
    grad_up = (grad_hidden * activated).astype(jnp.bfloat16)
    a_gate = jnp.dot(normed, pin_gate, preferred_element_type=jnp.float32)
    a_up = jnp.dot(normed, pin_up, preferred_element_type=jnp.float32)
    a_down = jnp.dot(hidden_act, pin_down, preferred_element_type=jnp.float32)
    b_gate = jnp.dot(grad_gate, pout_gate, preferred_element_type=jnp.float32)
    b_up = jnp.dot(grad_up, pout_up, preferred_element_type=jnp.float32)
    b_down = jnp.dot(out_grad, pout_down, preferred_element_type=jnp.float32)
    features = jnp.concatenate([project_pair(b_gate, a_gate), project_pair(b_up, a_up), project_pair(b_down, a_down)], axis=1)
    scores = jnp.dot(features, targets.T, precision=lax.Precision.HIGHEST, preferred_element_type=jnp.float32)
    return (features, scores)
```

```python
import functools
import jax
import jax.numpy as jnp
from jax import lax
from jax.experimental import pallas as pl
from jax.experimental.pallas import tpu as pltpu
from jax.sharding import PartitionSpec as P

SEQ = 64


EPSILON = 1e-05
F32 = jnp.float32
BF16 = jnp.bfloat16
CHIPS = 16
PAD = 128


def dot_nt(a, b):
    return lax.dot_general(a, b, (((1,), (1,)), ((), ())), preferred_element_type=F32)


def kernel(
    x_ref, g_ref, gain_ref, wg_hbm, wu_hbm, wd_hbm, pg_ref, pu_ref, qg_ref, qu_ref, pd_ref, qd_ref,
    out_ref,
    buf, wgu, wd, ss, gu_acc, h_acc, part, pair, own, rs,
    recv, send, w_sem, pair_sem, rs_send, rs_recv, ag_send, ag_recv, sib_send, sib_recv,
):
    me = lax.axis_index("tensor")
    z, y, x, c = me // 8, (me // 4) % 2, (me // 2) % 2, me % 2
    chip = me // 2
    sib = me + 1 - 2 * c
    width = x_ref.shape[1]
    tokens = x_ref.shape[0]
    half = tokens // 2
    hid = wg_hbm.shape[0]

    loads = [
        pltpu.make_async_copy(wg_hbm, wgu.at[pl.ds(0, hid)], w_sem.at[0]),
        pltpu.make_async_copy(wu_hbm, wgu.at[pl.ds(PAD, hid)], w_sem.at[1]),
        pltpu.make_async_copy(wd_hbm, wd, w_sem.at[2]),
    ]
    for load in loads:
        load.start()

    barrier = pltpu.get_barrier_semaphore()

    @pl.loop(1, CHIPS)
    def _(i):
        peer = ((chip + i) % CHIPS) * 2 + c
        pl.semaphore_signal(barrier, inc=1, device_id={"tensor": peer})

    pl.semaphore_signal(barrier, inc=1, device_id={"tensor": sib})
    buf[0, me] = x_ref[...]
    buf[1, me] = g_ref[...]
    pl.semaphore_wait(barrier, CHIPS)

    def dev(zz, fy, fx, cc):
        yy = 1 - y if fy else y
        xx = 1 - x if fx else x
        return ((zz * 2 + yy) * 2 + xx) * 2 + cc

    order = [
        z,
        jnp.where(z == 0, 1, z - 1),
        jnp.where(z == 0, 2, jnp.where(z == 3, 1, z + 1)),
        jnp.where(z < 2, 3, 0),
    ]
    counter = [0]
    pending = []

    def copy(a, h, owner, to, slot):
        block = buf.at[a, owner, pl.ds(h * half, half)]
        return pltpu.make_async_remote_copy(
            src_ref=block, dst_ref=block,
            send_sem=send.at[slot], recv_sem=recv.at[(a * 2 + h) * 32 + owner],
            device_id={"tensor": to},
        )

    def start(a, h, owner, to, cond=None):
        slot = counter[0]
        counter[0] += 1
        if cond is None:
            copy(a, h, owner, to, slot).start()
        else:
            @pl.when(cond)
            def _():
                copy(a, h, owner, to, slot).start()
        pending.append((a, h, owner, to, slot, cond))

    def arrive(a, h, owner):
        copy(a, h, owner, sib, 0).wait_recv()

    def flips(h, stage):
        if stage == 0:
            return [(0, 0)]
        if stage == 1:
            return [(0, 1)] if h == 0 else [(1, 0)]
        return [(1, 0), (1, 1)] if h == 0 else [(0, 1), (1, 1)]

    def lane_event(a, stage, k):
        for h in (0, 1):
            for fy, fx in flips(h, stage):
                owner = dev(order[k], fy, fx, c)
                if not (stage == 0 and k == 0):
                    arrive(a, h, owner)
                n1 = dev(z, 0, 1, c) if h == 0 else dev(z, 1, 0, c)
                n2 = dev(z, 1, 0, c) if h == 0 else dev(z, 0, 1, c)
                if stage == 0:
                    if k == 0:
                        start(a, h, owner, me + 8, z < 3)
                        start(a, h, owner, me - 8, z > 0)
                    elif k < 3:
                        up = order[k] < z
                        start(a, h, owner, jnp.where(up, me + 8, me - 8),
                              jnp.logical_or(jnp.logical_and(up, z < 3),
                                             jnp.logical_and(order[k] > z, z > 0)))
                    else:
                        up = order[k] < z
                        start(a, h, owner, jnp.where(up, me + 8, me - 8),
                              jnp.logical_or(jnp.logical_and(up, z < 3),
                                             jnp.logical_and(order[k] > z, z > 0)))
                    start(a, h, owner, n1)
                if stage < 2:
                    start(a, h, owner, n2)
                start(a, h, owner, sib)

    def sib_event(a, k):
        for h in (0, 1):
            for fy in (0, 1):
                for fx in (0, 1):
                    arrive(a, h, dev(order[k], fy, fx, 1 - c))

    def owner_of(k, i, cc):
        return (order[k] * 4 + i) * 2 + cc

    def squares(k, cc):
        @pl.loop(0, 4)
        def _(i):
            v = buf[0, owner_of(k, i, cc)].astype(F32)
            v = v * v
            ss[...] += v[:, :128] + v[:, 128:]

    def grads(k, cc):
        @pl.loop(0, 4)
        def _(i):
            owner = owner_of(k, i, cc)
            cols = pl.ds(pl.multiple_of(owner * width, width), width)
            h_acc[...] += dot_nt(buf[1, owner], wd[:, cols])

    def tick(a, t):
        work = squares if a == 0 else grads
        for stage in (0, 1, 2):
            k = t - stage
            if 0 <= k < 4:
                lane_event(a, stage, k)
        k = t - 2
        if 0 <= k < 4:
            work(k, c)
        k = t - 3
        if 0 <= k < 4:
            sib_event(a, k)
            work(k, 1 - c)

    def normed_of(owner):
        cols = pl.ds(pl.multiple_of(owner * width, width), width)
        scale = ss[:, 0:1]
        return (buf[0, owner].astype(F32) * scale * gain_ref[:, cols]).astype(BF16), cols

    def pre(lo, hi):
        @pl.loop(lo, hi)
        def _(owner):
            normed, cols = normed_of(owner)
            gu_acc[...] += dot_nt(normed, wgu[:, cols])

    ss[...] = jnp.zeros_like(ss)
    gu_acc[...] = jnp.zeros_like(gu_acc)
    h_acc[...] = jnp.zeros_like(h_acc)
    wgu[pl.ds(hid, PAD - hid)] = jnp.zeros((PAD - hid, wgu.shape[1]), BF16)
    wgu[pl.ds(PAD + hid, PAD - hid)] = jnp.zeros((PAD - hid, wgu.shape[1]), BF16)
    for t in (0, 1, 2, 3):
        tick(0, t)
        if t == 2:
            for load in loads:
                load.wait()
    tick(1, 0)
    tick(0, 4)
    tick(1, 1)
    tick(0, 5)
    tick(1, 2)
    tick(0, 6)
    total = jnp.sum(ss[...], axis=1, keepdims=True)
    ss[...] = jnp.broadcast_to(lax.rsqrt(total / (32 * width) + EPSILON), ss.shape)
    rank = pg_ref.shape[0]
    tick(1, 3)
    pre(0, 12)
    tick(1, 4)
    pre(12, 24)
    tick(1, 5)
    pre(24, 32)
    mine, _ = normed_of(me)
    part[:, 0:rank] = dot_nt(mine, pg_ref[...])
    part[:, rank:2 * rank] = dot_nt(mine, pu_ref[...])
    part[:, 2 * rank:3 * rank] = dot_nt(g_ref[...], qd_ref[...])
    gate_pre = gu_acc[:, 0:hid]
    up_pre = gu_acc[:, PAD:PAD + hid]
    sigmoid_gate = jax.nn.sigmoid(gate_pre)
    activated = gate_pre * sigmoid_gate
    hidden_act = (activated * up_pre).astype(BF16)
    part[:, 5 * rank:6 * rank] = dot_nt(hidden_act, pd_ref[...])
    tick(1, 6)
    grad_hidden = h_acc[...]
    grad_gate = (
        grad_hidden * up_pre * sigmoid_gate * (1.0 + gate_pre * (1.0 - sigmoid_gate))
    ).astype(BF16)
    grad_up = (grad_hidden * activated).astype(BF16)
    part[:, 3 * rank:4 * rank] = dot_nt(grad_gate, qg_ref[...])
    part[:, 4 * rank:5 * rank] = dot_nt(grad_up, qu_ref[...])

    swap = pltpu.make_async_remote_copy(
        src_ref=part.at[pl.ds(pl.multiple_of((1 - c) * half, half), half)], dst_ref=pair,
        send_sem=pair_sem.at[0], recv_sem=pair_sem.at[1], device_id={"tensor": sib},
    )
    swap.start()
    rows = half // CHIPS
    swap.wait_recv()
    own[...] = part[pl.ds(pl.multiple_of(c * half, half), half)] + pair[...]

    def scatter(i, to_me):
        j = (chip + i) % CHIPS
        slot = (chip + CHIPS - i) % CHIPS
        return pltpu.make_async_remote_copy(
            src_ref=own.at[pl.ds(pl.multiple_of(j * rows, rows), rows)],
            dst_ref=rs.at[slot if to_me else chip],
            send_sem=rs_send.at[i], recv_sem=rs_recv.at[i],
            device_id={"tensor": j * 2 + c},
        )

    @pl.loop(1, CHIPS)
    def _(i):
        scatter(i, False).start()

    rs[chip] = own[pl.ds(pl.multiple_of(chip * rows, rows), rows)]

    @pl.loop(1, CHIPS)
    def _(i):
        scatter(i, True).wait_recv()

    def place(ch, cc):
        return pl.ds(pl.multiple_of((cc * CHIPS + ch) * rows, rows), rows)

    out_ref[place(chip, c)] = jnp.sum(rs[...], axis=0)

    def spread(i, to_me):
        j = (chip + i) % CHIPS
        src = (chip + CHIPS - i) % CHIPS
        return pltpu.make_async_remote_copy(
            src_ref=out_ref.at[place(chip, c)],
            dst_ref=out_ref.at[place(src if to_me else chip, c)],
            send_sem=ag_send.at[i], recv_sem=ag_recv.at[i],
            device_id={"tensor": j * 2 + c},
        )

    def across(i, cc):
        src = (chip + CHIPS - i) % CHIPS
        return pltpu.make_async_remote_copy(
            src_ref=out_ref.at[place(src, cc)], dst_ref=out_ref.at[place(src, cc)],
            send_sem=sib_send.at[i], recv_sem=sib_recv.at[i], device_id={"tensor": sib},
        )

    @pl.loop(1, CHIPS)
    def _(i):
        spread(i, False).start()

    across(0, c).start()

    @pl.loop(1, CHIPS)
    def _(i):
        spread(i, True).wait_recv()
        across(i, c).start()

    @pl.loop(0, CHIPS)
    def _(i):
        across(i, 1 - c).wait_recv()

    for a, h, owner, to, slot, cond in pending:
        if cond is None:
            copy(a, h, owner, to, slot).wait_send()
        else:
            @pl.when(cond)
            def _(a=a, h=h, owner=owner, to=to, slot=slot):
                copy(a, h, owner, to, slot).wait_send()
    swap.wait_send()

    @pl.loop(1, CHIPS)
    def _(i):
        scatter(i, False).wait_send()
        spread(i, False).wait_send()

    @pl.loop(0, CHIPS)
    def _(i):
        across(i, c).wait_send()


N_SEND = 2 * 2 * (5 + 3 * 4 + 4 * 2 + 8)


def fused_sides(
    layer_input, out_grad, norm_gain, w_gate, w_up, w_down,
    pin_gate, pin_up, pout_gate, pout_up, pin_down, pout_down,
):
    tokens, width = layer_input.shape
    hid, d = w_gate.shape[1], w_gate.shape[0]
    rank = pin_gate.shape[1]
    vmem = pl.BlockSpec(memory_space=pltpu.VMEM)
    hbm = pl.BlockSpec(memory_space=pl.ANY)
    dma = pltpu.SemaphoreType.DMA
    return pl.pallas_call(
        kernel,
        out_shape=jax.ShapeDtypeStruct((tokens, 6 * rank), F32),
        in_specs=[vmem, vmem, vmem, hbm, hbm, hbm] + [vmem] * 6,
        out_specs=vmem,
        scratch_shapes=[
            pltpu.VMEM((2, 32, tokens, width), BF16),
            pltpu.VMEM((2 * PAD, d), BF16),
            pltpu.VMEM((hid, d), BF16),
            pltpu.VMEM((tokens, 128), F32),
            pltpu.VMEM((tokens, 2 * PAD), F32),
            pltpu.VMEM((tokens, hid), F32),
            pltpu.VMEM((tokens, 6 * rank), F32),
            pltpu.VMEM((tokens // 2, 6 * rank), F32),
            pltpu.VMEM((tokens // 2, 6 * rank), F32),
            pltpu.VMEM((CHIPS, tokens // 2 // CHIPS, 6 * rank), F32),
            dma((128,)), dma((N_SEND,)), dma((3,)), dma((2,)),
            dma((CHIPS,)), dma((CHIPS,)), dma((CHIPS,)), dma((CHIPS,)), dma((CHIPS,)), dma((CHIPS,)),
        ],
        compiler_params=pltpu.CompilerParams(
            collective_id=0, has_side_effects=True, vmem_limit_bytes=40 * 1024 * 1024
        ),
        cost_estimate=pl.CostEstimate(
            flops=6 * tokens * d * hid, bytes_accessed=6 * d * hid, transcendentals=tokens * hid
        ),
    )(
        layer_input, out_grad, norm_gain.reshape(1, -1), w_gate.T, w_up.T, w_down,
        pin_gate.T, pin_up.T, pout_gate.T, pout_up.T, pin_down.T, pout_down.T,
    )


def on_device_fused(*args):
    targets = args[-1]
    sides = fused_sides(*args[:-1])
    rank = sides.shape[1] // 6
    a_gate, a_up, b_down, b_gate, b_up, a_down = (
        sides[:, i * rank:(i + 1) * rank] for i in range(6)
    )
    features = jnp.concatenate(
        [project_pair(b_gate, a_gate), project_pair(b_up, a_up), project_pair(b_down, a_down)],
        axis=1,
    )
    scores = jnp.dot(
        features, targets.T, precision=lax.Precision.HIGHEST, preferred_element_type=jnp.float32
    )
    return (features, scores)


def project_pair(out_side, in_side):
    out_rows = out_side.reshape(-1, SEQ, out_side.shape[-1])
    in_rows = in_side.reshape(-1, SEQ, in_side.shape[-1])
    product = jnp.einsum("esi,esj->eij", out_rows, in_rows, precision=lax.Precision.HIGHEST)
    return product.reshape(product.shape[0], -1)


def on_device(
    layer_input,
    out_grad,
    norm_gain,
    w_gate,
    w_up,
    w_down,
    pin_gate,
    pin_up,
    pout_gate,
    pout_up,
    pin_down,
    pout_down,
    targets,
):
    shard_width = layer_input.shape[1]
    first_col = lax.axis_index("tensor") * shard_width
    gathered = lax.all_gather(layer_input, "tensor", axis=1, tiled=True)
    wide_rows = gathered.astype(jnp.float32)
    mean_square = jnp.mean(wide_rows * wide_rows, axis=-1, keepdims=True)
    normed = (wide_rows * lax.rsqrt(mean_square + EPSILON) * norm_gain).astype(jnp.bfloat16)
    normed_piece = lax.dynamic_slice_in_dim(normed, first_col, shard_width, 1)
    columns = normed
    gate_pre = jnp.dot(
        columns,
        lax.all_gather(w_gate, "dp", axis=0, tiled=True),
        preferred_element_type=jnp.float32,
    )
    up_pre = jnp.dot(
        columns, lax.all_gather(w_up, "dp", axis=0, tiled=True), preferred_element_type=jnp.float32
    )
    sigmoid_gate = jax.nn.sigmoid(gate_pre)
    activated = gate_pre * sigmoid_gate
    hidden_act = (activated * up_pre).astype(jnp.bfloat16)
    a_gate_part = jnp.dot(normed_piece, pin_gate, preferred_element_type=jnp.float32)
    a_up_part = jnp.dot(normed_piece, pin_up, preferred_element_type=jnp.float32)
    b_down_part = jnp.dot(out_grad, pout_down, preferred_element_type=jnp.float32)
    grad_rows = lax.all_gather(out_grad, "tensor", axis=1, tiled=True)
    columns = grad_rows
    grad_hidden = jnp.einsum(
        "td,hd->th",
        columns,
        lax.all_gather(w_down, "dp", axis=1, tiled=True),
        preferred_element_type=jnp.float32,
    )
    grad_gate = (
        grad_hidden * up_pre * sigmoid_gate * (1.0 + gate_pre * (1.0 - sigmoid_gate))
    ).astype(jnp.bfloat16)
    grad_up = (grad_hidden * activated).astype(jnp.bfloat16)
    b_gate_part = jnp.dot(grad_gate, pout_gate, preferred_element_type=jnp.float32)
    b_up_part = jnp.dot(grad_up, pout_up, preferred_element_type=jnp.float32)
    a_down_part = jnp.dot(hidden_act, pin_down, preferred_element_type=jnp.float32)
    a_gate, a_up, b_down, b_gate, b_up, a_down = lax.psum(
        (a_gate_part, a_up_part, b_down_part, b_gate_part, b_up_part, a_down_part), "tensor"
    )
    features = jnp.concatenate(
        [project_pair(b_gate, a_gate), project_pair(b_up, a_up), project_pair(b_down, a_down)],
        axis=1,
    )
    scores = jnp.dot(
        features, targets.T, precision=lax.Precision.HIGHEST, preferred_element_type=jnp.float32
    )
    return (features, scores)


def solution(mesh):
    fused = mesh.shape["tensor"] == 2 * CHIPS and mesh.shape["dp"] == 1 and mesh.shape["groups"] == 1
    return jax.shard_map(
        on_device_fused if fused else on_device,
        mesh=mesh,
        in_specs=(
            P(("groups", "dp"), "tensor"),
            P(("groups", "dp"), "tensor"),
            P(),
            P("dp", "tensor"),
            P("dp", "tensor"),
            P("tensor", "dp"),
            P("tensor", None),
            P("tensor", None),
            P("tensor", None),
            P("tensor", None),
            P("tensor", None),
            P("tensor", None),
            P("tensor", None),
        ),
        out_specs=(P(("groups", "dp"), None), P(("groups", "dp"), "tensor")),
        check_vma=False,
    )
```

```python
import functools
import jax
import jax.numpy as jnp
from jax import lax
from jax.experimental import pallas as pl
from jax.experimental.pallas import tpu as pltpu
from jax.sharding import PartitionSpec as P

SEQ = 64


EPSILON = 1e-05
F32 = jnp.float32
BF16 = jnp.bfloat16
CHIPS = 16
PAD = 128


def dot_nt(a, b):
    return lax.dot_general(a, b, (((1,), (1,)), ((), ())), preferred_element_type=F32)


def kernel(
    x_hbm, g_hbm, gain_hbm, wg_hbm, wu_hbm, wd_hbm, pg_hbm, pu_hbm, qg_hbm, qu_hbm, pd_hbm, qd_hbm,
    oute_ref, outl_ref,
    buf, wgu, wd, gate_factor, up_factor, gain_ref, pg_ref, pu_ref, qg_ref, qu_ref, pd_ref, qd_ref,
    ss, gu_acc, h_acc, part_e, pair_e, own_e, rs_e, part_l, pair_l, own_l, rs_l,
    recv, send, w_sem, pair_send, pair_recv, rs_send, rs_recv, ag_send, ag_recv, sib_send, sib_recv,
):
    me = lax.axis_index("tensor")
    z, y, x, c = me // 8, (me // 4) % 2, (me // 2) % 2, me % 2
    chip = me // 2
    sib = me + 1 - 2 * c
    tokens, width = x_hbm.shape
    half = tokens // 2
    hid = wg_hbm.shape[0]

    mine_in = [
        pltpu.make_async_copy(x_hbm, buf.at[0, me], w_sem.at[10]),
        pltpu.make_async_copy(g_hbm, buf.at[1, me], w_sem.at[11]),
    ]
    for load in mine_in:
        load.start()
    loads = [
        pltpu.make_async_copy(wg_hbm, wgu.at[pl.ds(0, hid)], w_sem.at[0]),
        pltpu.make_async_copy(wu_hbm, wgu.at[pl.ds(PAD, hid)], w_sem.at[1]),
        pltpu.make_async_copy(wd_hbm, wd, w_sem.at[2]),
        pltpu.make_async_copy(gain_hbm, gain_ref, w_sem.at[3]),
        pltpu.make_async_copy(pg_hbm, pg_ref, w_sem.at[4]),
        pltpu.make_async_copy(pu_hbm, pu_ref, w_sem.at[5]),
        pltpu.make_async_copy(qg_hbm, qg_ref, w_sem.at[6]),
        pltpu.make_async_copy(qu_hbm, qu_ref, w_sem.at[7]),
        pltpu.make_async_copy(pd_hbm, pd_ref, w_sem.at[8]),
        pltpu.make_async_copy(qd_hbm, qd_ref, w_sem.at[9]),
    ]
    for load in loads:
        load.start()

    barrier = pltpu.get_barrier_semaphore()

    @pl.loop(1, CHIPS)
    def _(i):
        peer = ((chip + i) % CHIPS) * 2 + c
        pl.semaphore_signal(barrier, inc=1, device_id={"tensor": peer})

    pl.semaphore_signal(barrier, inc=1, device_id={"tensor": sib})
    for load in mine_in:
        load.wait()
    pl.semaphore_wait(barrier, CHIPS)

    def dev(zz, fy, fx, cc):
        yy = 1 - y if fy else y
        xx = 1 - x if fx else x
        return ((zz * 2 + yy) * 2 + xx) * 2 + cc

    order = [
        z,
        jnp.where(z == 0, 1, z - 1),
        jnp.where(z == 0, 2, jnp.where(z == 3, 1, z + 1)),
        jnp.where(z < 2, 3, 0),
    ]
    counter = [0]
    pending = []

    def copy(a, h, owner, to, slot):
        block = buf.at[a, owner, pl.ds(h * half, half)]
        return pltpu.make_async_remote_copy(
            src_ref=block, dst_ref=block,
            send_sem=send.at[slot], recv_sem=recv.at[(a * 2 + h) * 32 + owner],
            device_id={"tensor": to},
        )

    def start(a, h, owner, to, cond=None):
        slot = counter[0]
        counter[0] += 1
        if cond is None:
            copy(a, h, owner, to, slot).start()
        else:
            @pl.when(cond)
            def _():
                copy(a, h, owner, to, slot).start()
        pending.append((a, h, owner, to, slot, cond))

    def arrive(a, h, owner):
        copy(a, h, owner, sib, 0).wait_recv()

    def flips(h, stage):
        if stage == 0:
            return [(0, 0)]
        if stage == 1:
            return [(0, 1)] if h == 0 else [(1, 0)]
        return [(1, 0), (1, 1)] if h == 0 else [(0, 1), (1, 1)]

    def lane_event(a, stage, k):
        for h in (0, 1):
            for fy, fx in flips(h, stage):
                owner = dev(order[k], fy, fx, c)
                if not (stage == 0 and k == 0):
                    arrive(a, h, owner)
                n1 = dev(z, 0, 1, c) if h == 0 else dev(z, 1, 0, c)
                n2 = dev(z, 1, 0, c) if h == 0 else dev(z, 0, 1, c)
                if stage == 0 or (stage == 1 and a == 1):
                    if k == 0:
                        start(a, h, owner, me + 8, z < 3)
                        start(a, h, owner, me - 8, z > 0)
                    else:
                        up = order[k] < z
                        start(a, h, owner, jnp.where(up, me + 8, me - 8),
                              jnp.logical_or(jnp.logical_and(up, z < 3),
                                             jnp.logical_and(order[k] > z, z > 0)))
                if stage == 0 and (a == 0 or k == 0):
                    start(a, h, owner, n1)
                if stage < 2:
                    start(a, h, owner, n2)
                start(a, h, owner, sib)

    def sib_event(a, k):
        for h in (0, 1):
            for fy in (0, 1):
                for fx in (0, 1):
                    arrive(a, h, dev(order[k], fy, fx, 1 - c))

    def owner_of(k, i, cc):
        return (order[k] * 4 + i) * 2 + cc

    def squares(k, cc):
        @pl.loop(0, 4)
        def _(i):
            v = buf[0, owner_of(k, i, cc)].astype(F32)
            v = v * v
            ss[...] += v[:, :128] + v[:, 128:]

    def grad_block(owner):
        cols = pl.ds(pl.multiple_of(owner * width, width), width)
        h_acc[...] += dot_nt(buf[1, owner], wd[:, cols])

    def grads(k, cc):
        @pl.loop(0, 4)
        def _(i):
            grad_block(owner_of(k, i, cc))

    def tick(a, t, between=None):
        work = squares if a == 0 else grads
        for stage in (0, 1, 2):
            k = t - stage
            if 0 <= k < 4:
                lane_event(a, stage, k)
                if between is not None:
                    between()
        k = t - 2
        if 0 <= k < 4:
            work(k, c)
        k = t - 3
        if 0 <= k < 4:
            sib_event(a, k)
            work(k, 1 - c)

    def normed_of(owner):
        cols = pl.ds(pl.multiple_of(owner * width, width), width)
        scale = ss[:, 0:1]
        return (buf[0, owner].astype(F32) * scale * gain_ref[:, cols]).astype(BF16), cols

    def pre(lo, hi):
        @pl.loop(lo, hi)
        def _(owner):
            normed, cols = normed_of(owner)
            gu_acc[...] += dot_nt(normed, wgu[:, cols])

    ss[...] = jnp.zeros_like(ss)
    gu_acc[...] = jnp.zeros_like(gu_acc)
    h_acc[...] = jnp.zeros_like(h_acc)
    wgu[pl.ds(hid, PAD - hid)] = jnp.zeros((PAD - hid, wgu.shape[1]), BF16)
    wgu[pl.ds(PAD + hid, PAD - hid)] = jnp.zeros((PAD - hid, wgu.shape[1]), BF16)
    for t in (0, 1, 2, 3):
        tick(0, t)
        if t == 2:
            for load in loads:
                load.wait()
    tick(1, 0)
    tick(0, 4)
    tick(1, 1)
    tick(0, 5)
    tick(1, 2)
    tick(0, 6)
    total = jnp.sum(ss[...], axis=1, keepdims=True)
    ss[...] = jnp.broadcast_to(lax.rsqrt(total / (32 * width) + EPSILON), ss.shape)
    rank = pg_ref.shape[0]
    done = [0]

    def some_pre(n=7):
        pre(done[0], min(done[0] + n, 32))
        done[0] = min(done[0] + n, 32)

    rows = half // CHIPS
    GROUPS = ((part_e, pair_e, own_e, rs_e, oute_ref), (part_l, pair_l, own_l, rs_l, outl_ref))

    def swap(g):
        part, pair = GROUPS[g][0], GROUPS[g][1]
        return pltpu.make_async_remote_copy(
            src_ref=part.at[pl.ds(pl.multiple_of((1 - c) * half, half), half)], dst_ref=pair,
            send_sem=pair_send.at[g], recv_sem=pair_recv.at[g], device_id={"tensor": sib},
        )

    def scatter(g, i, to_me):
        own, rs = GROUPS[g][2], GROUPS[g][3]
        j = (chip + i) % CHIPS
        slot = (chip + CHIPS - i) % CHIPS
        return pltpu.make_async_remote_copy(
            src_ref=own.at[pl.ds(pl.multiple_of(j * rows, rows), rows)],
            dst_ref=rs.at[slot if to_me else chip],
            send_sem=rs_send.at[g * CHIPS + i], recv_sem=rs_recv.at[g * CHIPS + i],
            device_id={"tensor": j * 2 + c},
        )

    def place(ch, cc):
        return pl.ds(pl.multiple_of((cc * CHIPS + ch) * rows, rows), rows)

    def spread(g, i, to_me):
        out = GROUPS[g][4]
        j = (chip + i) % CHIPS
        src = (chip + CHIPS - i) % CHIPS
        return pltpu.make_async_remote_copy(
            src_ref=out.at[place(chip, c)],
            dst_ref=out.at[place(src if to_me else chip, c)],
            send_sem=ag_send.at[g * CHIPS + i], recv_sem=ag_recv.at[g * CHIPS + i],
            device_id={"tensor": j * 2 + c},
        )

    def across(g, cc):
        block = GROUPS[g][4].at[pl.ds(pl.multiple_of(cc * half, half), half)]
        return pltpu.make_async_remote_copy(
            src_ref=block, dst_ref=block, send_sem=sib_send.at[g], recv_sem=sib_recv.at[g],
            device_id={"tensor": sib},
        )

    def start_scatter(g):
        part, pair, own, rs, _ = GROUPS[g]
        swap(g).wait_recv()
        own[...] = part[pl.ds(pl.multiple_of(c * half, half), half)] + pair[...]

        @pl.loop(1, CHIPS)
        def _(i):
            scatter(g, i, False).start()

        rs[chip] = own[pl.ds(pl.multiple_of(chip * rows, rows), rows)]

    def start_spread(g):
        @pl.loop(1, CHIPS)
        def _(i):
            scatter(g, i, True).wait_recv()

        GROUPS[g][4][place(chip, c)] = jnp.sum(GROUPS[g][3][...], axis=0)

        @pl.loop(1, CHIPS)
        def _(i):
            spread(g, i, False).start()

    def relay(g):
        @pl.loop(1, CHIPS)
        def _(i):
            spread(g, i, True).wait_recv()

        across(g, c).start()

    def finish(g):
        across(g, 1 - c).wait_recv()

    def drain(g):
        swap(g).wait_send()

        @pl.loop(1, CHIPS)
        def _(i):
            scatter(g, i, False).wait_send()
            spread(g, i, False).wait_send()

        across(g, c).wait_send()

    tick(1, 3, some_pre)
    some_pre(11)
    mine, _ = normed_of(me)
    part_e[:, 0:rank] = dot_nt(mine, pg_ref[...])
    part_e[:, rank:2 * rank] = dot_nt(mine, pu_ref[...])
    part_e[:, 2 * rank:3 * rank] = dot_nt(buf[1, me], qd_ref[...])
    gate_pre = gu_acc[:, 0:hid]
    up_pre = gu_acc[:, PAD:PAD + hid]
    sigmoid_gate = jax.nn.sigmoid(gate_pre)
    activated = gate_pre * sigmoid_gate
    hidden_act = (activated * up_pre).astype(BF16)
    part_e[:, 3 * rank:4 * rank] = dot_nt(hidden_act, pd_ref[...])
    swap(0).start()
    gate_factor[...] = up_pre * sigmoid_gate * (1.0 + gate_pre * (1.0 - sigmoid_gate))
    up_factor[...] = activated
    tick(1, 4)
    start_scatter(0)
    tick(1, 5)
    start_spread(0)
    for i in range(4):
        for h in (0, 1):
            arrive(1, h, owner_of(3, i, 1 - c))
        grad_block(owner_of(3, i, 1 - c))
    grad_hidden = h_acc[...]
    grad_gate = (grad_hidden * gate_factor[...]).astype(BF16)
    grad_up = (grad_hidden * up_factor[...]).astype(BF16)
    part_l[:, 0:rank] = dot_nt(grad_gate, qg_ref[...])
    part_l[:, rank:2 * rank] = dot_nt(grad_up, qu_ref[...])
    swap(1).start()
    start_scatter(1)
    relay(0)
    for a, h, owner, to, slot, cond in pending:
        if cond is None:
            copy(a, h, owner, to, slot).wait_send()
        else:
            @pl.when(cond)
            def _(a=a, h=h, owner=owner, to=to, slot=slot):
                copy(a, h, owner, to, slot).wait_send()
    start_spread(1)
    relay(1)
    finish(0)
    finish(1)
    drain(0)
    drain(1)


N_SEND = 2 * (33 + 35)


def fused_sides(
    layer_input, out_grad, norm_gain, w_gate, w_up, w_down,
    pin_gate, pin_up, pout_gate, pout_up, pin_down, pout_down,
):
    tokens, width = layer_input.shape
    hid, d = w_gate.shape[1], w_gate.shape[0]
    rank = pin_gate.shape[1]
    vmem = pl.BlockSpec(memory_space=pltpu.VMEM)
    hbm = pl.BlockSpec(memory_space=pl.ANY)
    dma = pltpu.SemaphoreType.DMA
    return pl.pallas_call(
        kernel,
        out_shape=[
            jax.ShapeDtypeStruct((tokens, 4 * rank), F32),
            jax.ShapeDtypeStruct((tokens, 2 * rank), F32),
        ],
        in_specs=[hbm] * 12,
        out_specs=[vmem, vmem],
        scratch_shapes=[
            pltpu.VMEM((2, 32, tokens, width), BF16),
            pltpu.VMEM((2 * PAD, d), BF16),
            pltpu.VMEM((hid, d), BF16),
            pltpu.VMEM((tokens, hid), F32),
            pltpu.VMEM((tokens, hid), F32),
            pltpu.VMEM((1, d), F32),
            pltpu.VMEM((rank, width), BF16),
            pltpu.VMEM((rank, width), BF16),
            pltpu.VMEM((rank, hid), BF16),
            pltpu.VMEM((rank, hid), BF16),
            pltpu.VMEM((rank, hid), BF16),
            pltpu.VMEM((rank, width), BF16),
            pltpu.VMEM((tokens, 128), F32),
            pltpu.VMEM((tokens, 2 * PAD), F32),
            pltpu.VMEM((tokens, hid), F32),
            pltpu.VMEM((tokens, 4 * rank), F32),
            pltpu.VMEM((tokens // 2, 4 * rank), F32),
            pltpu.VMEM((tokens // 2, 4 * rank), F32),
            pltpu.VMEM((CHIPS, tokens // 2 // CHIPS, 4 * rank), F32),
            pltpu.VMEM((tokens, 2 * rank), F32),
            pltpu.VMEM((tokens // 2, 2 * rank), F32),
            pltpu.VMEM((tokens // 2, 2 * rank), F32),
            pltpu.VMEM((CHIPS, tokens // 2 // CHIPS, 2 * rank), F32),
            dma((128,)), dma((N_SEND,)), dma((12,)), dma((2,)), dma((2,)),
        ] + [dma((2 * CHIPS,))] * 4 + [dma((2,))] * 2 + [
        ],
        compiler_params=pltpu.CompilerParams(
            collective_id=0, has_side_effects=True, vmem_limit_bytes=60 * 1024 * 1024
        ),
        cost_estimate=pl.CostEstimate(
            flops=6 * tokens * d * hid, bytes_accessed=6 * d * hid, transcendentals=tokens * hid
        ),
    )(
        layer_input, out_grad, norm_gain.reshape(1, -1), w_gate.T, w_up.T, w_down,
        pin_gate.T, pin_up.T, pout_gate.T, pout_up.T, pin_down.T, pout_down.T,
    )


def on_device_fused(*args):
    targets = args[-1]
    early, late = fused_sides(*args[:-1])
    rank = late.shape[1] // 2
    a_gate, a_up, b_down, a_down = (early[:, i * rank:(i + 1) * rank] for i in range(4))
    b_gate, b_up = late[:, :rank], late[:, rank:]
    features = jnp.concatenate(
        [project_pair(b_gate, a_gate), project_pair(b_up, a_up), project_pair(b_down, a_down)],
        axis=1,
    )
    scores = jnp.dot(
        features, targets.T, precision=lax.Precision.HIGHEST, preferred_element_type=jnp.float32
    )
    return (features, scores)


def project_pair(out_side, in_side):
    out_rows = out_side.reshape(-1, SEQ, out_side.shape[-1])
    in_rows = in_side.reshape(-1, SEQ, in_side.shape[-1])
    product = jnp.einsum("esi,esj->eij", out_rows, in_rows, precision=lax.Precision.HIGHEST)
    return product.reshape(product.shape[0], -1)


def on_device(
    layer_input,
    out_grad,
    norm_gain,
    w_gate,
    w_up,
    w_down,
    pin_gate,
    pin_up,
    pout_gate,
    pout_up,
    pin_down,
    pout_down,
    targets,
):
    shard_width = layer_input.shape[1]
    first_col = lax.axis_index("tensor") * shard_width
    gathered = lax.all_gather(layer_input, "tensor", axis=1, tiled=True)
    wide_rows = gathered.astype(jnp.float32)
    mean_square = jnp.mean(wide_rows * wide_rows, axis=-1, keepdims=True)
    normed = (wide_rows * lax.rsqrt(mean_square + EPSILON) * norm_gain).astype(jnp.bfloat16)
    normed_piece = lax.dynamic_slice_in_dim(normed, first_col, shard_width, 1)
    columns = normed
    gate_pre = jnp.dot(
        columns,
        lax.all_gather(w_gate, "dp", axis=0, tiled=True),
        preferred_element_type=jnp.float32,
    )
    up_pre = jnp.dot(
        columns, lax.all_gather(w_up, "dp", axis=0, tiled=True), preferred_element_type=jnp.float32
    )
    sigmoid_gate = jax.nn.sigmoid(gate_pre)
    activated = gate_pre * sigmoid_gate
    hidden_act = (activated * up_pre).astype(jnp.bfloat16)
    a_gate_part = jnp.dot(normed_piece, pin_gate, preferred_element_type=jnp.float32)
    a_up_part = jnp.dot(normed_piece, pin_up, preferred_element_type=jnp.float32)
    b_down_part = jnp.dot(out_grad, pout_down, preferred_element_type=jnp.float32)
    grad_rows = lax.all_gather(out_grad, "tensor", axis=1, tiled=True)
    columns = grad_rows
    grad_hidden = jnp.einsum(
        "td,hd->th",
        columns,
        lax.all_gather(w_down, "dp", axis=1, tiled=True),
        preferred_element_type=jnp.float32,
    )
    grad_gate = (
        grad_hidden * up_pre * sigmoid_gate * (1.0 + gate_pre * (1.0 - sigmoid_gate))
    ).astype(jnp.bfloat16)
    grad_up = (grad_hidden * activated).astype(jnp.bfloat16)
    b_gate_part = jnp.dot(grad_gate, pout_gate, preferred_element_type=jnp.float32)
    b_up_part = jnp.dot(grad_up, pout_up, preferred_element_type=jnp.float32)
    a_down_part = jnp.dot(hidden_act, pin_down, preferred_element_type=jnp.float32)
    a_gate, a_up, b_down, b_gate, b_up, a_down = lax.psum(
        (a_gate_part, a_up_part, b_down_part, b_gate_part, b_up_part, a_down_part), "tensor"
    )
    features = jnp.concatenate(
        [project_pair(b_gate, a_gate), project_pair(b_up, a_up), project_pair(b_down, a_down)],
        axis=1,
    )
    scores = jnp.dot(
        features, targets.T, precision=lax.Precision.HIGHEST, preferred_element_type=jnp.float32
    )
    return (features, scores)


def solution(mesh):
    fused = mesh.shape["tensor"] == 2 * CHIPS and mesh.shape["dp"] == 1 and mesh.shape["groups"] == 1
    return jax.shard_map(
        on_device_fused if fused else on_device,
        mesh=mesh,
        in_specs=(
            P(("groups", "dp"), "tensor"),
            P(("groups", "dp"), "tensor"),
            P(),
            P("dp", "tensor"),
            P("dp", "tensor"),
            P("tensor", "dp"),
            P("tensor", None),
            P("tensor", None),
            P("tensor", None),
            P("tensor", None),
            P("tensor", None),
            P("tensor", None),
            P("tensor", None),
        ),
        out_specs=(P(("groups", "dp"), None), P(("groups", "dp"), "tensor")),
        check_vma=False,
    )
```

```python
import functools
import jax
import jax.numpy as jnp
from jax import lax
from jax.experimental import pallas as pl
from jax.experimental.pallas import tpu as pltpu
from jax.sharding import PartitionSpec as P

SEQ = 64


EPSILON = 1e-05
F32 = jnp.float32
BF16 = jnp.bfloat16
CHIPS = 16
PAD = 128


def dot_nt(a, b):
    return lax.dot_general(a, b, (((1,), (1,)), ((), ())), preferred_element_type=F32)


def kernel(
    x_hbm, g_hbm, gain_hbm, wg_hbm, wu_hbm, wd_hbm, pg_hbm, pu_hbm, qg_hbm, qu_hbm, pd_hbm, qd_hbm,
    oute_ref, outl_ref,
    buf, wgu, wd, gate_factor, up_factor, gain_ref, pg_ref, pu_ref, qg_ref, qu_ref, pd_ref, qd_ref,
    ss, gu_acc, h_acc, part_e, pair_e, own_e, rs_e, part_l, pair_l, own_l, rs_l,
    recv, send, w_sem, pair_send, pair_recv, rs_send, rs_recv, ag_send, ag_recv, sib_send, sib_recv,
):
    me = lax.axis_index("tensor")
    z, y, x, c = me // 8, (me // 4) % 2, (me // 2) % 2, me % 2
    chip = me // 2
    sib = me + 1 - 2 * c
    tokens, width = x_hbm.shape
    half = tokens // 2
    hid = wg_hbm.shape[0]

    mine_in = [
        pltpu.make_async_copy(x_hbm, buf.at[0, me], w_sem.at[10]),
        pltpu.make_async_copy(g_hbm, buf.at[1, me], w_sem.at[11]),
    ]
    for load in mine_in:
        load.start()
    loads = [
        pltpu.make_async_copy(wg_hbm, wgu.at[pl.ds(0, hid)], w_sem.at[0]),
        pltpu.make_async_copy(wu_hbm, wgu.at[pl.ds(PAD, hid)], w_sem.at[1]),
        pltpu.make_async_copy(wd_hbm, wd, w_sem.at[2]),
        pltpu.make_async_copy(gain_hbm, gain_ref, w_sem.at[3]),
        pltpu.make_async_copy(pg_hbm, pg_ref, w_sem.at[4]),
        pltpu.make_async_copy(pu_hbm, pu_ref, w_sem.at[5]),
        pltpu.make_async_copy(qg_hbm, qg_ref, w_sem.at[6]),
        pltpu.make_async_copy(qu_hbm, qu_ref, w_sem.at[7]),
        pltpu.make_async_copy(pd_hbm, pd_ref, w_sem.at[8]),
        pltpu.make_async_copy(qd_hbm, qd_ref, w_sem.at[9]),
    ]
    for load in loads:
        load.start()

    barrier = pltpu.get_barrier_semaphore()

    @pl.loop(1, CHIPS)
    def _(i):
        peer = ((chip + i) % CHIPS) * 2 + c
        pl.semaphore_signal(barrier, inc=1, device_id={"tensor": peer})

    pl.semaphore_signal(barrier, inc=1, device_id={"tensor": sib})
    for load in mine_in:
        load.wait()
    pl.semaphore_wait(barrier, CHIPS)

    def dev(zz, fy, fx, cc):
        yy = 1 - y if fy else y
        xx = 1 - x if fx else x
        return ((zz * 2 + yy) * 2 + xx) * 2 + cc

    order = [
        z,
        jnp.where(z == 0, 1, z - 1),
        jnp.where(z == 0, 2, jnp.where(z == 3, 1, z + 1)),
        jnp.where(z < 2, 3, 0),
    ]
    counter = [0]
    pending = []

    def copy(a, h, owner, to, slot):
        block = buf.at[a, owner, pl.ds(h * half, half)]
        return pltpu.make_async_remote_copy(
            src_ref=block, dst_ref=block,
            send_sem=send.at[slot], recv_sem=recv.at[(a * 2 + h) * 32 + owner],
            device_id={"tensor": to},
        )

    def start(a, h, owner, to, cond=None):
        slot = counter[0]
        counter[0] += 1
        if cond is None:
            copy(a, h, owner, to, slot).start()
        else:
            @pl.when(cond)
            def _():
                copy(a, h, owner, to, slot).start()
        pending.append((a, h, owner, to, slot, cond))

    def arrive(a, h, owner):
        copy(a, h, owner, sib, 0).wait_recv()

    def flips(h, stage):
        if stage == 0:
            return [(0, 0)]
        if stage == 1:
            return [(0, 1)] if h == 0 else [(1, 0)]
        return [(1, 0), (1, 1)] if h == 0 else [(0, 1), (1, 1)]

    def lane_event(a, stage, k):
        for h in (0, 1):
            for fy, fx in flips(h, stage):
                owner = dev(order[k], fy, fx, c)
                if not (stage == 0 and k == 0):
                    arrive(a, h, owner)
                n1 = dev(z, 0, 1, c) if h == 0 else dev(z, 1, 0, c)
                n2 = dev(z, 1, 0, c) if h == 0 else dev(z, 0, 1, c)
                if stage == 0 or (stage == 1 and a == 0):
                    if k == 0:
                        start(a, h, owner, me + 8, z < 3)
                        start(a, h, owner, me - 8, z > 0)
                    else:
                        up = order[k] < z
                        start(a, h, owner, jnp.where(up, me + 8, me - 8),
                              jnp.logical_or(jnp.logical_and(up, z < 3),
                                             jnp.logical_and(order[k] > z, z > 0)))
                if stage == 0 and (a == 1 or k == 0):
                    start(a, h, owner, n1)
                if stage < 2:
                    start(a, h, owner, n2)
                start(a, h, owner, sib)

    def sib_event(a, k):
        for h in (0, 1):
            for fy in (0, 1):
                for fx in (0, 1):
                    arrive(a, h, dev(order[k], fy, fx, 1 - c))

    def owner_of(k, i, cc):
        return (order[k] * 4 + i) * 2 + cc

    def squares(k, cc):
        @pl.loop(0, 4)
        def _(i):
            v = buf[0, owner_of(k, i, cc)].astype(F32)
            v = v * v
            ss[...] += v[:, :128] + v[:, 128:]

    def grad_term(owner):
        cols = pl.ds(pl.multiple_of(owner * width, width), width)
        return dot_nt(buf[1, owner], wd[:, cols])

    def grads(k, cc):
        terms = [grad_term(owner_of(k, i, cc)) for i in range(4)]
        h_acc[...] += (terms[0] + terms[1]) + (terms[2] + terms[3])

    def tick(a, t, between=None):
        work = squares if a == 0 else grads
        for stage in (0, 1, 2):
            k = t - stage
            if 0 <= k < 4:
                lane_event(a, stage, k)
                if between is not None:
                    between()
        k = t - 2
        if 0 <= k < 4:
            work(k, c)
        k = t - 3
        if 0 <= k < 4:
            sib_event(a, k)
            work(k, 1 - c)

    def normed_of(owner):
        cols = pl.ds(pl.multiple_of(owner * width, width), width)
        scale = ss[:, 0:1]
        return (buf[0, owner].astype(F32) * scale * gain_ref[:, cols]).astype(BF16), cols

    def pre(lo, hi):
        @pl.loop(lo // 2, hi // 2)
        def _(pair):
            first, cols = normed_of(pair * 2)
            second, next_cols = normed_of(pair * 2 + 1)
            gu_acc[...] += dot_nt(first, wgu[:, cols]) + dot_nt(second, wgu[:, next_cols])

    ss[...] = jnp.zeros_like(ss)
    gu_acc[...] = jnp.zeros_like(gu_acc)
    h_acc[...] = jnp.zeros_like(h_acc)
    wgu[pl.ds(hid, PAD - hid)] = jnp.zeros((PAD - hid, wgu.shape[1]), BF16)
    wgu[pl.ds(PAD + hid, PAD - hid)] = jnp.zeros((PAD - hid, wgu.shape[1]), BF16)
    for t in (0, 1, 2, 3):
        tick(0, t)
        if t == 2:
            for load in loads:
                load.wait()
    tick(1, 0)
    tick(0, 4)
    tick(1, 1)
    tick(0, 5)
    tick(1, 2)
    tick(0, 6)
    total = jnp.sum(ss[...], axis=1, keepdims=True)
    ss[...] = jnp.broadcast_to(lax.rsqrt(total / (32 * width) + EPSILON), ss.shape)
    rank = pg_ref.shape[0]
    done = [0]

    def some_pre(n=8):
        pre(done[0], min(done[0] + n, 32))
        done[0] = min(done[0] + n, 32)

    rows = half // CHIPS
    GROUPS = ((part_e, pair_e, own_e, rs_e, oute_ref), (part_l, pair_l, own_l, rs_l, outl_ref))

    def swap(g):
        part, pair = GROUPS[g][0], GROUPS[g][1]
        return pltpu.make_async_remote_copy(
            src_ref=part.at[pl.ds(pl.multiple_of((1 - c) * half, half), half)], dst_ref=pair,
            send_sem=pair_send.at[g], recv_sem=pair_recv.at[g], device_id={"tensor": sib},
        )

    def scatter(g, i, to_me):
        own, rs = GROUPS[g][2], GROUPS[g][3]
        j = (chip + i) % CHIPS
        slot = (chip + CHIPS - i) % CHIPS
        return pltpu.make_async_remote_copy(
            src_ref=own.at[pl.ds(pl.multiple_of(j * rows, rows), rows)],
            dst_ref=rs.at[slot if to_me else chip],
            send_sem=rs_send.at[g * CHIPS + i], recv_sem=rs_recv.at[g * CHIPS + i],
            device_id={"tensor": j * 2 + c},
        )

    def place(ch, cc):
        return pl.ds(pl.multiple_of((cc * CHIPS + ch) * rows, rows), rows)

    def spread(g, i, to_me):
        out = GROUPS[g][4]
        j = (chip + i) % CHIPS
        src = (chip + CHIPS - i) % CHIPS
        return pltpu.make_async_remote_copy(
            src_ref=out.at[place(chip, c)],
            dst_ref=out.at[place(src if to_me else chip, c)],
            send_sem=ag_send.at[g * CHIPS + i], recv_sem=ag_recv.at[g * CHIPS + i],
            device_id={"tensor": j * 2 + c},
        )

    def across(g, cc):
        block = GROUPS[g][4].at[pl.ds(pl.multiple_of(cc * half, half), half)]
        return pltpu.make_async_remote_copy(
            src_ref=block, dst_ref=block, send_sem=sib_send.at[g], recv_sem=sib_recv.at[g],
            device_id={"tensor": sib},
        )

    def start_scatter(g):
        part, pair, own, rs, _ = GROUPS[g]
        swap(g).wait_recv()
        own[...] = part[pl.ds(pl.multiple_of(c * half, half), half)] + pair[...]

        @pl.loop(1, CHIPS)
        def _(i):
            scatter(g, i, False).start()

        rs[chip] = own[pl.ds(pl.multiple_of(chip * rows, rows), rows)]

    def start_spread(g):
        @pl.loop(1, CHIPS)
        def _(i):
            scatter(g, i, True).wait_recv()

        GROUPS[g][4][place(chip, c)] = jnp.sum(GROUPS[g][3][...], axis=0)

        @pl.loop(1, CHIPS)
        def _(i):
            spread(g, i, False).start()

    def relay(g):
        @pl.loop(1, CHIPS)
        def _(i):
            spread(g, i, True).wait_recv()

        across(g, c).start()

    def finish(g):
        across(g, 1 - c).wait_recv()

    def drain(g):
        swap(g).wait_send()

        @pl.loop(1, CHIPS)
        def _(i):
            scatter(g, i, False).wait_send()
            spread(g, i, False).wait_send()

        across(g, c).wait_send()

    tick(1, 3, some_pre)
    some_pre()
    mine, _ = normed_of(me)
    part_e[:, 0:rank] = dot_nt(mine, pg_ref[...])
    part_e[:, rank:2 * rank] = dot_nt(mine, pu_ref[...])
    part_e[:, 2 * rank:3 * rank] = dot_nt(buf[1, me], qd_ref[...])
    gate_pre = gu_acc[:, 0:hid]
    up_pre = gu_acc[:, PAD:PAD + hid]
    sigmoid_gate = jax.nn.sigmoid(gate_pre)
    activated = gate_pre * sigmoid_gate
    hidden_act = (activated * up_pre).astype(BF16)
    part_e[:, 3 * rank:4 * rank] = dot_nt(hidden_act, pd_ref[...])
    swap(0).start()
    gate_factor[...] = up_pre * sigmoid_gate * (1.0 + gate_pre * (1.0 - sigmoid_gate))
    up_factor[...] = activated
    tick(1, 4)
    start_scatter(0)
    tick(1, 5)
    start_spread(0)
    for i in range(4):
        for h in (0, 1):
            arrive(1, h, owner_of(3, i, 1 - c))
        h_acc[...] += grad_term(owner_of(3, i, 1 - c))
    grad_hidden = h_acc[...]
    grad_gate = (grad_hidden * gate_factor[...]).astype(BF16)
    grad_up = (grad_hidden * up_factor[...]).astype(BF16)
    part_l[:, 0:rank] = dot_nt(grad_gate, qg_ref[...])
    part_l[:, rank:2 * rank] = dot_nt(grad_up, qu_ref[...])
    swap(1).start()
    start_scatter(1)
    relay(0)
    for a, h, owner, to, slot, cond in pending:
        if cond is None:
            copy(a, h, owner, to, slot).wait_send()
        else:
            @pl.when(cond)
            def _(a=a, h=h, owner=owner, to=to, slot=slot):
                copy(a, h, owner, to, slot).wait_send()
    start_spread(1)
    relay(1)
    finish(0)
    finish(1)
    drain(0)
    drain(1)


N_SEND = 2 * (33 + 35)


def fused_sides(
    layer_input, out_grad, norm_gain, w_gate, w_up, w_down,
    pin_gate, pin_up, pout_gate, pout_up, pin_down, pout_down,
):
    tokens, width = layer_input.shape
    hid, d = w_gate.shape[1], w_gate.shape[0]
    rank = pin_gate.shape[1]
    vmem = pl.BlockSpec(memory_space=pltpu.VMEM)
    hbm = pl.BlockSpec(memory_space=pl.ANY)
    dma = pltpu.SemaphoreType.DMA
    return pl.pallas_call(
        kernel,
        out_shape=[
            jax.ShapeDtypeStruct((tokens, 4 * rank), F32),
            jax.ShapeDtypeStruct((tokens, 2 * rank), F32),
        ],
        in_specs=[hbm] * 12,
        out_specs=[vmem, vmem],
        scratch_shapes=[
            pltpu.VMEM((2, 32, tokens, width), BF16),
            pltpu.VMEM((2 * PAD, d), BF16),
            pltpu.VMEM((hid, d), BF16),
            pltpu.VMEM((tokens, hid), F32),
            pltpu.VMEM((tokens, hid), F32),
            pltpu.VMEM((1, d), F32),
            pltpu.VMEM((rank, width), BF16),
            pltpu.VMEM((rank, width), BF16),
            pltpu.VMEM((rank, hid), BF16),
            pltpu.VMEM((rank, hid), BF16),
            pltpu.VMEM((rank, hid), BF16),
            pltpu.VMEM((rank, width), BF16),
            pltpu.VMEM((tokens, 128), F32),
            pltpu.VMEM((tokens, 2 * PAD), F32),
            pltpu.VMEM((tokens, hid), F32),
            pltpu.VMEM((tokens, 4 * rank), F32),
            pltpu.VMEM((tokens // 2, 4 * rank), F32),
            pltpu.VMEM((tokens // 2, 4 * rank), F32),
            pltpu.VMEM((CHIPS, tokens // 2 // CHIPS, 4 * rank), F32),
            pltpu.VMEM((tokens, 2 * rank), F32),
            pltpu.VMEM((tokens // 2, 2 * rank), F32),
            pltpu.VMEM((tokens // 2, 2 * rank), F32),
            pltpu.VMEM((CHIPS, tokens // 2 // CHIPS, 2 * rank), F32),
            dma((128,)), dma((N_SEND,)), dma((12,)), dma((2,)), dma((2,)),
        ] + [dma((2 * CHIPS,))] * 4 + [dma((2,))] * 2 + [
        ],
        compiler_params=pltpu.CompilerParams(
            collective_id=0, has_side_effects=True, vmem_limit_bytes=60 * 1024 * 1024
        ),
        cost_estimate=pl.CostEstimate(
            flops=6 * tokens * d * hid, bytes_accessed=6 * d * hid, transcendentals=tokens * hid
        ),
    )(
        layer_input, out_grad, norm_gain.reshape(1, -1), w_gate.T, w_up.T, w_down,
        pin_gate.T, pin_up.T, pout_gate.T, pout_up.T, pin_down.T, pout_down.T,
    )


def on_device_fused(*args):
    targets = args[-1]
    early, late = fused_sides(*args[:-1])
    rank = late.shape[1] // 2
    a_gate, a_up, b_down, a_down = (early[:, i * rank:(i + 1) * rank] for i in range(4))
    b_gate, b_up = late[:, :rank], late[:, rank:]
    features = jnp.concatenate(
        [project_pair(b_gate, a_gate), project_pair(b_up, a_up), project_pair(b_down, a_down)],
        axis=1,
    )
    scores = jnp.dot(
        features, targets.T, precision=lax.Precision.HIGHEST, preferred_element_type=jnp.float32
    )
    return (features, scores)


def project_pair(out_side, in_side):
    out_rows = out_side.reshape(-1, SEQ, out_side.shape[-1])
    in_rows = in_side.reshape(-1, SEQ, in_side.shape[-1])
    product = jnp.einsum("esi,esj->eij", out_rows, in_rows, precision=lax.Precision.HIGHEST)
    return product.reshape(product.shape[0], -1)


def on_device(
    layer_input,
    out_grad,
    norm_gain,
    w_gate,
    w_up,
    w_down,
    pin_gate,
    pin_up,
    pout_gate,
    pout_up,
    pin_down,
    pout_down,
    targets,
):
    shard_width = layer_input.shape[1]
    first_col = lax.axis_index("tensor") * shard_width
    gathered = lax.all_gather(layer_input, "tensor", axis=1, tiled=True)
    wide_rows = gathered.astype(jnp.float32)
    mean_square = jnp.mean(wide_rows * wide_rows, axis=-1, keepdims=True)
    normed = (wide_rows * lax.rsqrt(mean_square + EPSILON) * norm_gain).astype(jnp.bfloat16)
    normed_piece = lax.dynamic_slice_in_dim(normed, first_col, shard_width, 1)
    columns = normed
    gate_pre = jnp.dot(
        columns,
        lax.all_gather(w_gate, "dp", axis=0, tiled=True),
        preferred_element_type=jnp.float32,
    )
    up_pre = jnp.dot(
        columns, lax.all_gather(w_up, "dp", axis=0, tiled=True), preferred_element_type=jnp.float32
    )
    sigmoid_gate = jax.nn.sigmoid(gate_pre)
    activated = gate_pre * sigmoid_gate
    hidden_act = (activated * up_pre).astype(jnp.bfloat16)
    a_gate_part = jnp.dot(normed_piece, pin_gate, preferred_element_type=jnp.float32)
    a_up_part = jnp.dot(normed_piece, pin_up, preferred_element_type=jnp.float32)
    b_down_part = jnp.dot(out_grad, pout_down, preferred_element_type=jnp.float32)
    grad_rows = lax.all_gather(out_grad, "tensor", axis=1, tiled=True)
    columns = grad_rows
    grad_hidden = jnp.einsum(
        "td,hd->th",
        columns,
        lax.all_gather(w_down, "dp", axis=1, tiled=True),
        preferred_element_type=jnp.float32,
    )
    grad_gate = (
        grad_hidden * up_pre * sigmoid_gate * (1.0 + gate_pre * (1.0 - sigmoid_gate))
    ).astype(jnp.bfloat16)
    grad_up = (grad_hidden * activated).astype(jnp.bfloat16)
    b_gate_part = jnp.dot(grad_gate, pout_gate, preferred_element_type=jnp.float32)
    b_up_part = jnp.dot(grad_up, pout_up, preferred_element_type=jnp.float32)
    a_down_part = jnp.dot(hidden_act, pin_down, preferred_element_type=jnp.float32)
    a_gate, a_up, b_down, b_gate, b_up, a_down = lax.psum(
        (a_gate_part, a_up_part, b_down_part, b_gate_part, b_up_part, a_down_part), "tensor"
    )
    features = jnp.concatenate(
        [project_pair(b_gate, a_gate), project_pair(b_up, a_up), project_pair(b_down, a_down)],
        axis=1,
    )
    scores = jnp.dot(
        features, targets.T, precision=lax.Precision.HIGHEST, preferred_element_type=jnp.float32
    )
    return (features, scores)


def solution(mesh):
    fused = mesh.shape["tensor"] == 2 * CHIPS and mesh.shape["dp"] == 1 and mesh.shape["groups"] == 1
    return jax.shard_map(
        on_device_fused if fused else on_device,
        mesh=mesh,
        in_specs=(
            P(("groups", "dp"), "tensor"),
            P(("groups", "dp"), "tensor"),
            P(),
            P("dp", "tensor"),
            P("dp", "tensor"),
            P("tensor", "dp"),
            P("tensor", None),
            P("tensor", None),
            P("tensor", None),
            P("tensor", None),
            P("tensor", None),
            P("tensor", None),
            P("tensor", None),
        ),
        out_specs=(P(("groups", "dp"), None), P(("groups", "dp"), "tensor")),
        check_vma=False,
    )
```
